32 devices in a mesh: parts: 2 (over x), ep: 16 (over z, y, core).
Axes of the slice: x: 2, y: 2, z: 4, core: 2. Of those that a mesh axis runs over, the one named last changes fastest.
Arguments:
- tokens: bfloat16 [1, 256, 7168], P(None, ('parts', 'ep')), parts along dimension 1, may hold values from -6 to 6
- expert_ids: int32 [1, 256, 2], P(None, ('parts', 'ep')), parts along dimension 1, may hold values from 0 to 7, all different within a row; in each aligned block of 8 rows (0 to 7, 8 to 15, ..., all dimensions but the last counted through in order) at most 4 rows name the same one
- gate_weights: float32 [1, 256, 2], P(None, ('parts', 'ep')), parts along dimension 1, may hold values from 0.2 to 1
- w_gate: bfloat16 [16, 7168, 512], P('ep'), may hold values from -0.0625 to 0.0625
- scale_gate: bfloat16 [16, 56, 512], P('ep'), may hold values from 0.5 to 2
- w_up: bfloat16 [16, 7168, 512], P('ep'), may hold values from -0.0625 to 0.0625
- scale_up: bfloat16 [16, 56, 512], P('ep'), may hold values from 0.5 to 2
- w_down: bfloat16 [16, 512, 7168], P('ep'), may hold values from -0.1875 to 0.1875
- scale_down: bfloat16 [16, 4, 7168], P('ep'), may hold values from 0.5 to 2
- outlier_cols: int32 [8, 128], replicated, may hold values from 0 to 7167
- outlier_gate: bfloat16 [16, 128, 512], P('ep'), may hold values from -0.5 to 0.5
- outlier_up: bfloat16 [16, 128, 512], P('ep'), may hold values from -0.5 to 0.5
- shared_gate: bfloat16 [16, 7168, 512], P('ep'), as said below
- shared_up: bfloat16 [16, 7168, 512], P('ep'), as said below
- shared_down: bfloat16 [16, 512, 7168], P('ep'), as said below
Outputs:
- mixed: bfloat16 [1, 256, 7168], P(None, ('parts', 'ep')), parts along dimension 1
The draws below stay inside these ranges and needn't reach their ends.
There are 2 independent parts, one for each index of `parts`. The reference program is written for one: setup_inputs(seed, part) draws one part's arguments, and reference() takes and returns one part's arrays. A program takes and returns all parts, laid end to end along the dimension named above; an argument that names none is the same for every part. Nothing has to cross between parts.
Inputs may be any that keep to these rules, and one draw needn't show every extreme that they name: `expert_ids`: each row names 2 different experts; among the rows of one device in one step no expert is named by more than 4 rows, and in some device's rows some expert is named exactly 4 times. `outlier_cols`: feature indices; an expert may repeat one. `shared_gate`: slices s and s + 2 are equal. `shared_up`: slices s and s + 2 are equal. `shared_down`: slices s and s + 2 are equal.
All inputs are finite; a program needn't handle non-finite values.
Results may differ from the reference program's by a relative error of at most 0.007.
Values may be sent and summed in bfloat16 or wider, within the bound.
No kernel may reach another device: no remote copies, remote signals or barrier semaphores. Data moves between devices by JAX's collectives and lax.ppermute only.
A program may use at most 192 MiB of HBM per device.

```python
import math
import jax
import jax.numpy as jnp
import numpy as np
from jax import lax

D = 7168
FF = 1024
SFF = 1024
TOPK = 2
OUTL = 128
QBLOCK = 128
STEPS = 1
ROWS_DEV = 8
GROUP = 2
EXPERTS = 8
HID = 512
SHID = 512
CAP = 4
ROWS = 128
N_EP = 16


def shared_slices(key, height, breadth, fan):
    base = jax.random.normal(key, (GROUP, height, breadth), jnp.float32) * fan ** (-0.5)
    return jnp.tile(base, (EXPERTS, 1, 1))


def draw_shared_gate(key, part):
    key = jax.random.fold_in(key, 21)
    return shared_slices(key, D, SHID, D).astype(jnp.bfloat16)


def draw_shared_up(key, part):
    key = jax.random.fold_in(key, 22)
    return shared_slices(key, D, SHID, D).astype(jnp.bfloat16)


def draw_shared_down(key, part):
    key = jax.random.fold_in(key, 23)
    return shared_slices(key, SHID, D, SFF).astype(jnp.bfloat16)


def with_ends(entries, rng, smallest, largest):
    longest = entries.shape.index(max(entries.shape))
    spots = []
    for shift in (0, 1):
        where = [jax.random.randint(jax.random.fold_in(rng, axis), (), 0, length) for axis, length in enumerate(entries.shape)]
        where[longest] = (where[longest] + shift) % entries.shape[longest]
        spots.append(tuple(where))
    return entries.at[spots[0]].set(smallest).at[spots[1]].set(largest)


def block_scale(stream_key, dims, shards, low, top_value):
    loudness, own = 1.0, jax.random.fold_in(stream_key, 6)
    for dim, blocks in shards:
        steps = jnp.exp(jax.random.uniform(jax.random.fold_in(own, dim), (blocks,), jnp.float32, low / len(shards), top_value / len(shards)))
        loudness = loudness * jnp.repeat(steps, dims[dim] // blocks).reshape([-1 if axis == dim else 1 for axis in range(len(dims))])
    return loudness


def deal_out(rng, own, number, rows, amount, top, bound, skew):
    ranking = jax.random.permutation(rng, amount)
    heavy_load, common = load_shares(amount, rows * top, bound, skew, True), load_shares(amount, rows * top, bound, skew, False)
    places = jnp.arange(amount)

    def named(sizes, offset_by):
        used = int((sizes > 0).sum())
        fixed = max(1, used // 4)
        shifted = fixed + (places - fixed + offset_by * (used - fixed)) % max(1, amount - fixed)
        return jnp.zeros((amount,), jnp.int32).at[ranking[jnp.where(places < fixed, places, shifted)]].set(jnp.asarray(sizes, jnp.int32))

    sizes = jnp.where(number % 4 == 0, named(heavy_load, number // 4), named(common, number - number // 4 - 1))
    mixed = jax.random.permutation(jax.random.fold_in(own, 3), amount)
    donor, taker = mixed[0:amount // 2 * 2:2], mixed[1:amount // 2 * 2:2]
    margin = jnp.minimum(sizes[donor] - 1, bound - sizes[taker]) // 2
    margin = jnp.where((donor == ranking[0]) | (taker == ranking[0]) | (sizes[taker] == 0), 0, jnp.maximum(margin, 0))
    shifted = jax.random.randint(jax.random.fold_in(own, 4), (amount // 2,), 0, 1 << 20) % (margin + 1)
    sizes = sizes.at[donor].add(-shifted).at[taker].add(shifted)
    labels = jnp.searchsorted(jnp.cumsum(sizes), jnp.arange(rows * top), side="right").astype(jnp.int32)
    table = labels.reshape(top, rows).T
    table = table[jax.random.permutation(jax.random.fold_in(own, 1), rows)]
    offset_by = jax.random.randint(jax.random.fold_in(own, 2), (rows, 1), 0, top)
    return jnp.take_along_axis(table, (jnp.arange(top)[None, :] + offset_by) % top, axis=1)


def load_shares(count, total, reach, slope, full):
    weights = [(1 << 20) // math.isqrt(grade ** slope) + 1 for grade in range(1, count + 1)]
    largest = reach if full else min(reach, max(-(-total // count), total * weights[0] // sum(weights)))
    least = 1 if total - largest >= count - 1 else 0
    counts, rest = [largest] + [least] * (count - 1), total - largest - least * (count - 1)
    while rest > 0:
        free = [i for i in range(1, count) if counts[i] < largest] or [i for i in range(1, count) if counts[i] < reach]
        mass, remaining = sum([weights[i] for i in free]), rest
        for i in free:
            addition = min(reach - counts[i], max(1, remaining * weights[i] // mass), rest)
            counts[i] = counts[i] + addition
            rest = rest - addition
    return np.array(counts)


def noise(key, shape, scale, reach, split=(), kind=jnp.bfloat16):
    values = scale * jax.random.normal(key, shape, jnp.float32)
    if split:
        values = values * block_scale(key, shape, split, -0.22, 0.18)
    return jnp.clip(values, -reach, reach).astype(kind)


def setup_inputs(seed: int = 0, part: int = 0) -> dict:
    streams_of = jax.random.split(jax.random.key(seed), 16)
    part_splits = jax.random.split(jax.random.fold_in(streams_of[15], part), 16)
    tokens = noise(part_splits[0], (STEPS, ROWS, D), 1.0, 6.0, ((1, 16),))
    expert_ids_keys = jax.random.split(jax.random.fold_in(part_splits[1], 1), STEPS * ROWS // ROWS_DEV)
    expert_ids_turns = jax.random.permutation(jax.random.fold_in(part_splits[1], 3), STEPS * ROWS // ROWS_DEV)
    expert_ids = jax.vmap(lambda own, number: deal_out(jax.random.fold_in(part_splits[1], 2), own, number, ROWS_DEV, EXPERTS, TOPK, CAP, 2))(expert_ids_keys, expert_ids_turns).reshape((STEPS, ROWS, TOPK))
    gate_weights = jnp.clip(0.2 + 0.8 * jax.random.uniform(part_splits[2], (STEPS, ROWS, TOPK), jnp.float32) ** block_scale(part_splits[2], (STEPS, ROWS, TOPK), ((1, 16),), -0.2, 0.2), 0.2, 1.0)
    w_gate = noise(streams_of[3], (N_EP, D, HID), D ** -0.5, 0.0625, ((0, 16),))
    scale_gate = jnp.clip(jnp.exp(math.log(2.0) - 1.3862944 * jax.random.uniform(streams_of[4], (N_EP, D // QBLOCK, HID), jnp.float32) ** block_scale(streams_of[4], (N_EP, D // QBLOCK, HID), ((0, 16),), -0.2, 0.2)), 0.5, 2.0).astype(jnp.bfloat16)
    w_up = noise(streams_of[5], (N_EP, D, HID), D ** -0.5, 0.0625, ((0, 16),))
    scale_up = jnp.clip(jnp.exp(math.log(2.0) - 1.3862944 * jax.random.uniform(streams_of[6], (N_EP, D // QBLOCK, HID), jnp.float32) ** block_scale(streams_of[6], (N_EP, D // QBLOCK, HID), ((0, 16),), -0.2, 0.2)), 0.5, 2.0).astype(jnp.bfloat16)
    w_down = noise(streams_of[7], (N_EP, HID, D), FF ** -0.5, 0.1875, ((0, 16),))
    scale_down = jnp.clip(jnp.exp(math.log(2.0) - 1.3862944 * jax.random.uniform(streams_of[8], (N_EP, HID // QBLOCK, D), jnp.float32) ** block_scale(streams_of[8], (N_EP, HID // QBLOCK, D), ((0, 16),), -0.2, 0.2)), 0.5, 2.0).astype(jnp.bfloat16)
    outlier_cols = with_ends(jax.random.randint(streams_of[9], (EXPERTS, OUTL), 0, D), jax.random.fold_in(streams_of[9], 1), 0, D - 1).astype(jnp.int32)
    outlier_gate = noise(streams_of[10], (N_EP, OUTL, HID), OUTL ** -0.5, 0.5, ((0, 16),))
    outlier_up = noise(streams_of[11], (N_EP, OUTL, HID), OUTL ** -0.5, 0.5, ((0, 16),))
    shared_gate = draw_shared_gate(jax.random.fold_in(streams_of[15], 71), part)
    shared_up = draw_shared_up(jax.random.fold_in(streams_of[15], 71), part)
    shared_down = draw_shared_down(jax.random.fold_in(streams_of[15], 71), part)
    return {"tokens": tokens, "expert_ids": expert_ids, "gate_weights": gate_weights, "w_gate": w_gate, "scale_gate": scale_gate, "w_up": w_up, "scale_up": scale_up, "w_down": w_down, "scale_down": scale_down, "outlier_cols": outlier_cols, "outlier_gate": outlier_gate, "outlier_up": outlier_up, "shared_gate": shared_gate, "shared_up": shared_up, "shared_down": shared_down}


def matmul32(left, right):
    return jnp.dot(left.astype(jnp.float32), right.astype(jnp.float32), precision=lax.Precision.HIGHEST, preferred_element_type=jnp.float32)


def dequant(codes, scales):
    height, breadth = codes.shape
    blocks = scales.shape[0]
    scaled = codes.astype(jnp.float32).reshape(blocks, height // blocks, breadth) * scales.astype(jnp.float32)[:, None, :]
    return scaled.reshape(height, breadth).astype(jnp.bfloat16)


def split_inputs(inputs, columns):
    width = inputs.shape[-1]
    hits = jnp.any(jnp.arange(width, dtype=jnp.int32)[None, :] == columns[:, None], axis=0)
    masked = jnp.where(hits[None, :], jnp.zeros((), inputs.dtype), inputs)
    picked = jnp.take(inputs, columns, axis=1)
    return masked, picked


def join_columns(slices):
    return slices.transpose(1, 0, 2).reshape(slices.shape[1], slices.shape[0] * slices.shape[2])


def shared_feed(inputs, gate_matrix, up_matrix, down_matrix):
    gate_val = matmul32(inputs, gate_matrix)
    up_val = matmul32(inputs, up_matrix)
    hidden = (jax.nn.silu(gate_val) * up_val).astype(jnp.bfloat16)
    return matmul32(hidden, down_matrix)


def grouped(array):
    return array.reshape((EXPERTS, GROUP) + array.shape[1:])


def reference(tokens, expert_ids, gate_weights, w_gate, scale_gate, w_up, scale_up, w_down, scale_down, outlier_cols, outlier_gate, outlier_up, shared_gate, shared_up, shared_down):
    shared_gate_whole = join_columns(shared_gate[:GROUP])
    shared_up_whole = join_columns(shared_up[:GROUP])
    shared_down_whole = shared_down[:GROUP].reshape(SFF, D)
    limit = N_EP * CAP
    packs = (jnp.arange(EXPERTS, dtype=jnp.int32), grouped(w_gate), grouped(scale_gate), grouped(w_up), grouped(scale_up), grouped(w_down), grouped(scale_down), outlier_cols, grouped(outlier_gate), grouped(outlier_up))
    results = []
    for step_index in range(STEPS):
        current = tokens[step_index]
        routed_ids = expert_ids[step_index]
        weights = gate_weights[step_index]

        def one_expert(total, pack):
            expert, gate_codes, gate_scales, up_codes, up_scales, down_codes, down_scales, columns, extra_gate, extra_up = pack
            gate_matrix = join_columns(jax.vmap(dequant)(gate_codes, gate_scales))
            up_matrix = join_columns(jax.vmap(dequant)(up_codes, up_scales))
            down_slices = jax.vmap(dequant)(down_codes, down_scales)
            hit_mask = routed_ids == expert
            row_weight = jnp.sum(jnp.where(hit_mask, weights, 0.0), axis=1)
            chosen = jnp.any(hit_mask, axis=1)
            index = jnp.nonzero(chosen, size=limit, fill_value=0)[0].astype(jnp.int32)
            live = jnp.arange(limit, dtype=jnp.int32) < jnp.sum(chosen.astype(jnp.int32))
            picked_rows = current[index]
            masked, outliers = split_inputs(picked_rows, columns)
            gate_val = matmul32(masked, gate_matrix) + matmul32(outliers, join_columns(extra_gate))
            up_val = matmul32(masked, up_matrix) + matmul32(outliers, join_columns(extra_up))
            hidden = (jax.nn.silu(gate_val) * up_val).astype(jnp.bfloat16)
            per_slice = jnp.einsum("ngh,ghd->gnd", hidden.reshape(limit, GROUP, HID).astype(jnp.float32), down_slices.astype(jnp.float32), precision=lax.Precision.HIGHEST)
            rounded = lax.optimization_barrier(per_slice.astype(jnp.bfloat16))
            result = jnp.sum(rounded.astype(jnp.float32), axis=0)
            scale = jnp.where(live, row_weight[index], 0.0)
            return total.at[index].add(scale[:, None] * result), None

        routed, unused = lax.scan(one_expert, jnp.zeros((ROWS, D), jnp.float32), packs)
        shared_out = shared_feed(current, shared_gate_whole, shared_up_whole, shared_down_whole)
        results.append((routed + shared_out).astype(jnp.bfloat16))
    return jnp.stack(results, axis=0)
```

```python
import functools

import jax
import jax.numpy as jnp
from jax import lax
from jax.experimental import pallas as pl
from jax.experimental.pallas import tpu as pltpu
from jax.sharding import PartitionSpec as P

FF = 1024
TOPK = 2
TILE = 16
BF16 = jnp.bfloat16
F32 = jnp.float32
VMEM = pl.BlockSpec(memory_space=pltpu.VMEM)
ANY = pl.BlockSpec(memory_space=pl.ANY)
SMEM = pl.BlockSpec(memory_space=pltpu.SMEM)


def params(mib):
    return pltpu.CompilerParams(vmem_limit_bytes=mib << 20)


def cost(flops, nbytes):
    return pl.CostEstimate(flops=int(flops), bytes_accessed=int(nbytes), transcendentals=0)


def matmul(left, right):
    return jnp.dot(left, right, preferred_element_type=F32)


def in_hbm(array):
    return pltpu.with_memory_space_constraint(array, pltpu.HBM)


def iota(shape, dim):
    return lax.broadcasted_iota(jnp.int32, shape, dim)


def slot_codes(ids_ref, home, rows, capacity):
    ids = [ids_ref[t, r] for r in range(rows) for t in range(TOPK)]
    codes = []
    for n, e in enumerate(ids):
        place = jnp.int32(0)
        for earlier in ids[:n]:
            place += (earlier == e).astype(jnp.int32)
        codes.append((e ^ home) * capacity + place)
    return codes


def by_row(values, position, rows, choice):
    out = jnp.zeros(position.shape, values[0].dtype)
    for r in range(rows):
        out = jnp.where(position == r, values[r * TOPK + choice], out)
    return out


def send_kernel(cap, order, ids_ref, home_ref, tokens_hbm, *refs):
    blocks, (tokens_ref, stacked, sem) = refs[:-3], refs[-3:]
    copy = pltpu.make_async_copy(tokens_hbm, tokens_ref, sem)
    copy.start()
    rows = tokens_ref.shape[0]
    parts = TILE // cap
    width = tokens_ref.shape[1] // parts
    codes = slot_codes(ids_ref, home_ref[0], rows, cap)
    shape = (len(blocks) * TILE, parts * rows)
    j, lane = iota(shape, 0), iota(shape, 1)
    code = j // TILE * cap + j % cap
    same = j % TILE // cap == lane // rows
    position = iota((1, parts * rows), 1) % rows
    hit = jnp.zeros(shape, F32)
    for t in range(TOPK):
        hit += jnp.where(same & (code == by_row(codes, position, rows, t)), 1.0, 0.0)
    copy.wait()
    for q in range(parts):
        stacked[q * rows : (q + 1) * rows, :] = tokens_ref[
            :, q * width : (q + 1) * width
        ].astype(F32)
    chosen = matmul(hit.astype(BF16), stacked[...].astype(BF16)).astype(BF16)
    for m, block in zip(order, blocks):
        block[...] = chosen[m * TILE : (m + 1) * TILE]


def sorted_blocks(order, refs):
    return [refs[order.index(m)] for m in range(len(order))]


def unpack_kernel(cap, order, *refs):
    blocks, out = sorted_blocks(order, refs[:-1]), refs[-1]
    count, parts = len(blocks), TILE // cap
    slots, width = count * cap, blocks[0].shape[1]
    shape = (parts * slots, count * TILE)
    i, j = iota(shape, 0), iota(shape, 1)
    source = i % slots // cap * TILE + i // slots * cap + i % cap
    arranged = matmul(
        jnp.where(source == j, 1.0, 0.0).astype(BF16),
        jnp.concatenate([b[...] for b in blocks], axis=0),
    ).astype(BF16)
    for q in range(parts):
        out[:, q * width : (q + 1) * width] = arranged[q * slots : (q + 1) * slots]


def pack_kernel(cap, order, mine_ref, other_ref, *blocks):
    count, parts = len(blocks), TILE // cap
    slots, width = count * cap, mine_ref.shape[1] // parts
    total = (mine_ref[...].astype(F32) + other_ref[...].astype(F32)).astype(BF16)
    shape = (count * TILE, parts * slots)
    j, i = iota(shape, 0), iota(shape, 1)
    source = j % TILE // cap * slots + j // TILE * cap + j % cap
    arranged = matmul(
        jnp.where(source == i, 1.0, 0.0).astype(BF16),
        jnp.concatenate([total[:, q * width : (q + 1) * width] for q in range(parts)], axis=0),
    ).astype(BF16)
    for m, block in zip(order, blocks):
        block[...] = arranged[m * TILE : (m + 1) * TILE]


def prepare_kernel(
    step, tall, wg, wu, wd, sg, su, sd, cols, gate, up, down, onehot, keep, gate_scale, up_scale, sems
):
    chunks = wg.shape[0] // step
    block = wg.shape[0] // sg.shape[0]
    heights = wd.shape[0] // tall

    def moved(k, source, target, start, size):
        here = pl.ds(start, size)
        return pltpu.make_async_copy(source.at[here], target.at[here], sems.at[k])

    gates = [moved(c, wg, gate, c * step, step) for c in range(chunks)]
    ups = [moved(chunks + c, wu, up, c * step, step) for c in range(chunks)]
    downs = [moved(2 * chunks + c, wd, down, c * tall, tall) for c in range(heights)]
    for c in range(chunks):
        gates[c].start()
        ups[c].start()
    for copy in downs:
        copy.start()

    gate_scale[...] = sg[...].astype(F32)
    up_scale[...] = su[...].astype(F32)
    outliers = cols.shape[1]
    for c in range(chunks):
        here = slice(c * step, (c + 1) * step)
        hot = jnp.where(iota((step, outliers), 0) + c * step == cols[...], 1.0, 0.0).astype(BF16)
        onehot[here, :] = hot
        count = lax.dot_general(
            jnp.ones((8, outliers), BF16), hot, (((1,), (1,)), ((), ())), preferred_element_type=F32
        )
        keep[:, here] = jnp.where(count == 0.0, 1.0, 0.0)

    for c in range(chunks):
        for copy, target, scale in ((gates[c], gate, gate_scale), (ups[c], up, up_scale)):
            copy.wait()

            @pl.loop(0, step // block)
            def _(b):
                n = c * (step // block) + b
                here = pl.ds(pl.multiple_of(n * block, block), block)
                factor = scale[pl.ds(n, 1), :].astype(BF16)
                target[here, :] = target[here, :] * jnp.broadcast_to(factor, (block, factor.shape[1]))

    unit = wd.shape[0] // sd.shape[0]
    for c in range(heights):
        downs[c].wait()
        n = c * tall // unit
        factor = sd[...].astype(F32)[n : n + 1, :].astype(BF16)

        @pl.loop(0, tall // TILE)
        def _(b):
            here = pl.ds(pl.multiple_of(c * tall + b * TILE, TILE), TILE)
            down[here, :] = down[here, :] * jnp.broadcast_to(factor, (TILE, factor.shape[1]))


def expert_kernel(chunk, wide, gate, up, down, onehot, keep, extra_gate, extra_up, *refs):
    count = (len(refs) - 4) // 2
    pieces, outs = refs[:count], refs[count : 2 * count]
    gate_acc, up_acc, picked, hidden_ref = refs[2 * count :]
    height = pieces[0].shape[0]
    gate_acc[...] = jnp.zeros_like(gate_acc)
    up_acc[...] = jnp.zeros_like(up_acc)
    picked[...] = jnp.zeros_like(picked)

    @pl.loop(0, gate.shape[0] // chunk)
    def _(i):
        here = pl.ds(pl.multiple_of(i * chunk, chunk), chunk)
        whole = jnp.concatenate([piece[:, here] for piece in pieces], axis=0)
        kept = keep[:, here][0:1].astype(BF16)
        masked = whole * jnp.broadcast_to(kept, whole.shape)
        picked[...] += matmul(whole, onehot[here, :])
        gate_acc[...] += matmul(masked, gate[here, :])
        up_acc[...] += matmul(masked, up[here, :])

    outliers = picked[...].astype(BF16)
    gate_val = gate_acc[...] + matmul(outliers, extra_gate[...])
    up_val = up_acc[...] + matmul(outliers, extra_up[...])
    hidden_ref[...] = (gate_val / (1.0 + jnp.exp(-gate_val)) * up_val).astype(BF16)

    @pl.loop(0, down.shape[1] // wide)
    def _(i):
        here = pl.ds(pl.multiple_of(i * wide, wide), wide)
        result = matmul(hidden_ref[...], down[:, here]).astype(BF16)
        for n, out in enumerate(outs):
            out[:, here] = result[n * height : (n + 1) * height]


def shared_kernel(step, tall, wide, wg, wu, wd, *refs):
    count = (len(refs) - 8) // 2
    pieces, outs = refs[:count], refs[count : 2 * count]
    gate, up, down, rows_ref, gate_acc, up_acc, hidden_ref, sems = refs[2 * count :]
    height = pieces[0].shape[0]
    chunks, heights = wg.shape[0] // step, wd.shape[0] // tall

    def moved(k, source, target, start, size):
        here = pl.ds(start, size)
        return pltpu.make_async_copy(source.at[here], target.at[here], sems.at[k])

    gates = [moved(c, wg, gate, c * step, step) for c in range(chunks)]
    ups = [moved(chunks + c, wu, up, c * step, step) for c in range(chunks)]
    downs = [moved(2 * chunks + c, wd, down, c * tall, tall) for c in range(heights)]
    for c in range(chunks):
        gates[c].start()
        ups[c].start()
    for copy in downs:
        copy.start()
    rows_ref[...] = jnp.concatenate([p[...].astype(F32) for p in pieces], axis=0).astype(BF16)
    gate_acc[...] = jnp.zeros_like(gate_acc)
    up_acc[...] = jnp.zeros_like(up_acc)
    for c in range(chunks):
        here = slice(c * step, (c + 1) * step)
        gates[c].wait()
        gate_acc[...] += matmul(rows_ref[:, here], gate[here, :])
        ups[c].wait()
        up_acc[...] += matmul(rows_ref[:, here], up[here, :])
    value = gate_acc[...]
    hidden_ref[...] = (value / (1.0 + jnp.exp(-value)) * up_acc[...]).astype(BF16)
    for copy in downs:
        copy.wait()

    @pl.loop(0, down.shape[1] // wide)
    def _(i):
        here = pl.ds(pl.multiple_of(i * wide, wide), wide)
        result = matmul(hidden_ref[...], down[:, here])
        for n, out in enumerate(outs):
            out[:, here] = result[n * height : (n + 1) * height].astype(out.dtype)


def combine_kernel(cap, order, ids_ref, home_ref, weights_ref, mine_ref, other_ref, *refs):
    blocks, out = sorted_blocks(order, refs[:-1]), refs[-1]
    rows = out.shape[0]
    parts = TILE // cap
    width = out.shape[1] // parts
    codes = slot_codes(ids_ref, home_ref[0], rows, cap)
    weights = [weights_ref[t, r] for r in range(rows) for t in range(TOPK)]
    shape = (parts * rows, len(blocks) * TILE)
    i, j = iota(shape, 0), iota(shape, 1)
    code = j // TILE * cap + j % cap
    same = j % TILE // cap == i // rows
    position = iota((parts * rows, 1), 0) % rows
    share = jnp.zeros(shape, F32)
    for t in range(TOPK):
        share += jnp.where(
            same & (code == by_row(codes, position, rows, t)),
            by_row(weights, position, rows, t),
            0.0,
        )
    high = share.astype(BF16)
    rest = share - high.astype(F32)
    middle = rest.astype(BF16)
    low = (rest - middle.astype(F32)).astype(BF16)
    arrived = jnp.concatenate([b[...] for b in blocks], axis=0)
    routed = matmul(high, arrived) + matmul(middle, arrived) + matmul(low, arrived)
    for q in range(parts):
        here = slice(q * width, (q + 1) * width)
        shared = mine_ref[:, here].astype(F32)
        for n in range(other_ref.shape[0] // rows):
            shared += other_ref[n * rows : (n + 1) * rows, here].astype(F32)
        out[:, here] = (routed[q * rows : (q + 1) * rows] + shared).astype(out.dtype)


def on_device(
    tokens,
    expert_ids,
    gate_weights,
    w_gate,
    scale_gate,
    w_up,
    scale_up,
    w_down,
    scale_down,
    outlier_cols,
    outlier_gate,
    outlier_up,
    shared_gate,
    shared_up,
    shared_down,
):
    devices = lax.axis_size("ep")
    device = lax.axis_index("ep")
    hid = w_gate.shape[2]
    group = FF // hid
    experts = devices // group
    bits = group.bit_length() - 1
    rows, width = tokens.shape[1], tokens.shape[2]
    cap = max(2, rows * TOPK * 2 // experts)
    home = device // group
    block = width // scale_gate.shape[1]
    part_width = width * cap // TILE
    slots = experts * cap

    def swap(array, mask):
        return lax.ppermute(array, "ep", [(d, d ^ mask) for d in range(devices)])

    def spread(pieces):
        for bit in range(bits):
            pieces = pieces + [swap(piece, 1 << bit) for piece in pieces]
        return pieces

    current, ids = tokens[0], expert_ids[0].T
    home_ref = home.astype(jnp.int32).reshape(1)
    send_block = jax.ShapeDtypeStruct((TILE, part_width), BF16)
    order = (0,) + tuple(sorted(range(1, experts), key=lambda m: (-m.bit_length(), m)))

    blocks = pl.pallas_call(
        functools.partial(send_kernel, cap, order),
        in_specs=[SMEM, SMEM, ANY],
        out_specs=[VMEM] * experts,
        out_shape=[send_block] * experts,
        scratch_shapes=[
            pltpu.VMEM((rows, width), BF16),
            pltpu.VMEM((TILE // cap * rows, part_width), F32),
            pltpu.SemaphoreType.DMA,
        ],
        compiler_params=params(8),
        cost_estimate=cost(1e8, 1e6),
        name="send",
    )(ids, home_ref, in_hbm(current))
    arrived = [blocks[0]] + [swap(block, m * group) for m, block in zip(order[1:], blocks[1:])]

    cols, _ = lax.optimization_barrier(
        (lax.dynamic_slice_in_dim(outlier_cols, home, 1, 0), blocks[0])
    )
    step, tall = 1024, hid // scale_down.shape[1]
    copies = 2 * (width // step) + hid // tall
    stored = jax.ShapeDtypeStruct((width, hid), BF16)
    prepared = pl.pallas_call(
        functools.partial(prepare_kernel, step, tall),
        in_specs=[ANY] * 3 + [VMEM] * 4,
        out_specs=[VMEM] * 5,
        out_shape=[
            stored,
            stored,
            jax.ShapeDtypeStruct((hid, width), BF16),
            jax.ShapeDtypeStruct((width, outlier_cols.shape[1]), BF16),
            jax.ShapeDtypeStruct((8, width), F32),
        ],
        scratch_shapes=[
            pltpu.VMEM(scale_gate.shape[1:], F32),
            pltpu.VMEM(scale_up.shape[1:], F32),
            pltpu.SemaphoreType.DMA((copies,)),
        ],
        compiler_params=params(12),
        cost_estimate=cost(1e9, 6 * hid * width),
        name="prepare",
    )(
        in_hbm(w_gate[0]),
        in_hbm(w_up[0]),
        in_hbm(w_down[0]),
        scale_gate[0],
        scale_up[0],
        scale_down[0],
        cols,
    )
    arrived, keep = lax.optimization_barrier((tuple(arrived), prepared[4]))
    prepared = list(prepared[:4]) + [keep]

    whole = jax.ShapeDtypeStruct((slots, width), BF16)
    taken = pl.pallas_call(
        functools.partial(unpack_kernel, cap, order),
        in_specs=[VMEM] * experts,
        out_specs=VMEM,
        out_shape=whole,
        compiler_params=params(16),
        cost_estimate=cost(1e8, 1e6),
        name="unpack",
    )(*arrived)
    pieces = spread([taken])

    partials = pl.pallas_call(
        functools.partial(expert_kernel, 1024, 1024),
        in_specs=[VMEM] * (7 + group),
        out_specs=[VMEM] * group,
        out_shape=[whole] * group,
        scratch_shapes=[
            pltpu.VMEM((group * slots, hid), F32),
            pltpu.VMEM((group * slots, hid), F32),
            pltpu.VMEM((group * slots, outlier_cols.shape[1]), F32),
            pltpu.VMEM((group * slots, hid), BF16),
        ],
        compiler_params=params(12),
        cost_estimate=cost(6 * group * slots * width * hid, 6 * hid * width),
        name="expert",
    )(*prepared, outlier_gate[0], outlier_up[0], *pieces)

    for bit in reversed(range(1, bits)):
        half = 1 << bit
        partials = [
            (mine.astype(F32) + swap(other, half).astype(F32)).astype(BF16)
            for mine, other in zip(partials[:half], partials[half:])
        ]
    returning = pl.pallas_call(
        functools.partial(pack_kernel, cap, order),
        in_specs=[VMEM] * 2,
        out_specs=[VMEM] * experts,
        out_shape=[send_block] * experts,
        compiler_params=params(16),
        cost_estimate=cost(1e8, 1e6),
        name="pack",
    )(partials[0], swap(partials[1], 1))
    returned = [returning[0]] + [swap(block, m * group) for m, block in zip(order[1:], returning[1:])]

    row_pieces = spread([current])
    row_pieces = list(lax.optimization_barrier((tuple(row_pieces), returning[0]))[0])
    shared = pl.pallas_call(
        functools.partial(shared_kernel, step, tall, 1024),
        in_specs=[ANY] * 3 + [VMEM] * group,
        out_specs=[VMEM] * group,
        out_shape=[jax.ShapeDtypeStruct((rows, width), F32)]
        + [jax.ShapeDtypeStruct((rows, width), BF16)] * (group - 1),
        scratch_shapes=[
            pltpu.VMEM((width, hid), BF16),
            pltpu.VMEM((width, hid), BF16),
            pltpu.VMEM((hid, width), BF16),
            pltpu.VMEM((group * rows, width), BF16),
            pltpu.VMEM((group * rows, hid), F32),
            pltpu.VMEM((group * rows, hid), F32),
            pltpu.VMEM((group * rows, hid), BF16),
            pltpu.SemaphoreType.DMA((copies,)),
        ],
        compiler_params=params(32),
        cost_estimate=cost(6 * group * rows * width * hid, 6 * hid * width),
        name="shared",
    )(in_hbm(shared_gate[0]), in_hbm(shared_up[0]), in_hbm(shared_down[0]), *row_pieces)
    others = [swap(shared[n], n) for n in range(1, group)]
    others = others[0] if group == 2 else jnp.concatenate(others, axis=0)

    out = pl.pallas_call(
        functools.partial(combine_kernel, cap, order),
        in_specs=[SMEM, SMEM, SMEM] + [VMEM] * (2 + experts),
        out_specs=VMEM,
        out_shape=jax.ShapeDtypeStruct((rows, width), BF16),
        compiler_params=params(16),
        cost_estimate=cost(1e8, 1e6),
        name="combine",
    )(ids, home_ref, gate_weights[0].T, shared[0], others, *returned)
    return out[None]


def solution(mesh):
    rows = P(None, ("parts", "ep"), None)
    held = P("ep", None, None)
    placed = (rows, rows, rows) + (held,) * 6 + (P(),) + (held,) * 5
    return jax.shard_map(
        on_device, mesh=mesh, in_specs=placed, out_specs=rows, check_vma=False
    )
```

```python
import functools

import jax
import jax.numpy as jnp
from jax import lax
from jax.experimental import pallas as pl
from jax.experimental.pallas import tpu as pltpu
from jax.sharding import PartitionSpec as P

FF = 1024
TOPK = 2
TILE = 16
BF16 = jnp.bfloat16
F32 = jnp.float32
VMEM = pl.BlockSpec(memory_space=pltpu.VMEM)
ANY = pl.BlockSpec(memory_space=pl.ANY)
SMEM = pl.BlockSpec(memory_space=pltpu.SMEM)


def params(mib):
    return pltpu.CompilerParams(vmem_limit_bytes=mib << 20)


def cost(flops, nbytes):
    return pl.CostEstimate(flops=int(flops), bytes_accessed=int(nbytes), transcendentals=0)


def matmul(left, right):
    return jnp.dot(left, right, preferred_element_type=F32)


def in_hbm(array):
    return pltpu.with_memory_space_constraint(array, pltpu.HBM)


def iota(shape, dim):
    return lax.broadcasted_iota(jnp.int32, shape, dim)


def slot_codes(ids_ref, home, rows, capacity):
    ids = [ids_ref[t, r] for r in range(rows) for t in range(TOPK)]
    codes = []
    for n, e in enumerate(ids):
        place = jnp.int32(0)
        for earlier in ids[:n]:
            place += (earlier == e).astype(jnp.int32)
        apart = e ^ home
        codes.append(jnp.where(apart & 1 == 0, (apart >> 1) * capacity + place, -1))
    return codes


def block_codes(block, slot, capacity, masks):
    code = jnp.zeros(block.shape, jnp.int32)
    for n, mask in enumerate(masks):
        code = jnp.where(block == n, mask // 2 * capacity, code)
    return code + slot


def by_row(values, position, rows, choice):
    out = jnp.zeros(position.shape, values[0].dtype)
    for r in range(rows):
        out = jnp.where(position == r, values[r * TOPK + choice], out)
    return out


def choose_kernel(cap, masks, rows, own_ids, neighbour_ids, home_ref, out):
    parts = TILE // cap
    span = parts * rows
    shape = (out.shape[0], span)
    j, lane = iota(shape, 0), iota(shape, 1)
    code = block_codes(j // (2 * TILE), j % cap, cap, masks)
    same = j % TILE // cap == lane // rows
    position = iota((1, span), 1) % rows
    for n, ids in enumerate((own_ids, neighbour_ids)):
        codes = slot_codes(ids, home_ref[0], rows, cap)
        here = same & (j // TILE % 2 == n)
        hit = jnp.zeros(shape, F32)
        for t in range(TOPK):
            hit += jnp.where(here & (code == by_row(codes, position, rows, t)), 1.0, 0.0)
        out[:, n * span : (n + 1) * span] = hit


def send_kernel(cap, hit_ref, own_hbm, neighbour, *refs):
    blocks, (own, stacked, sem) = refs[:-3], refs[-3:]
    copy = pltpu.make_async_copy(own_hbm, own, sem)
    copy.start()
    rows = own.shape[0]
    parts = TILE // cap
    width = own.shape[1] // parts
    for n, tokens in ((1, neighbour), (0, own)):
        if n == 0:
            copy.wait()
        for q in range(parts):
            start = (n * parts + q) * rows
            stacked[start : start + rows, :] = tokens[:, q * width : (q + 1) * width].astype(F32)
    chosen = matmul(hit_ref[...].astype(BF16), stacked[...].astype(BF16)).astype(BF16)
    for m, block in enumerate(blocks):
        block[...] = chosen[2 * m * TILE : 2 * (m + 1) * TILE]


def unpack_kernel(cap, *refs):
    blocks, out = refs[:-1], refs[-1]
    parts, slots, width = TILE // cap, out.shape[0], blocks[0].shape[1]
    shape = (parts * slots, slots // cap * TILE)
    i, j = iota(shape, 0), iota(shape, 1)
    source = i % slots // cap * TILE + i // slots * cap + i % cap
    arranged = matmul(
        jnp.where(source == j, 1.0, 0.0).astype(BF16),
        jnp.concatenate([b[...] for b in blocks], axis=0),
    ).astype(BF16)
    for q in range(parts):
        out[:, q * width : (q + 1) * width] = arranged[q * slots : (q + 1) * slots]


def pack_kernel(cap, mine_ref, other_ref, *blocks):
    parts, slots = TILE // cap, mine_ref.shape[0]
    width = mine_ref.shape[1] // parts
    total = (mine_ref[...].astype(F32) + other_ref[...].astype(F32)).astype(BF16)
    shape = (slots // cap * TILE, parts * slots)
    j, i = iota(shape, 0), iota(shape, 1)
    source = j % TILE // cap * slots + j // TILE * cap + j % cap
    arranged = matmul(
        jnp.where(source == i, 1.0, 0.0).astype(BF16),
        jnp.concatenate([total[:, q * width : (q + 1) * width] for q in range(parts)], axis=0),
    ).astype(BF16)
    start = 0
    for block in blocks:
        block[...] = arranged[start : start + block.shape[0]]
        start += block.shape[0]


def moved(source, target, sems, k, start, size, units=None):
    here = pl.ds(start, size)
    source = source.at[here] if units is None else source.at[here, units]
    return pltpu.make_async_copy(source, target.at[here], sems.at[k])


def load_kernel(step, half_ref, wg, wu, sg, su, sd, cols, gate, up, s_gate, s_up, s_down, onehot, keep, sems):
    chunks = wg.shape[0] // step
    units = s_gate.shape[1]
    split = units < wg.shape[1]
    used = pl.ds(pl.multiple_of(half_ref[0] * units, units), units) if split else None
    copies = []
    for pairs, part in ((((wg, gate), (wu, up)), None), (((sg, s_gate), (su, s_up)), used)):
        for c in range(chunks):
            for source, target in pairs:
                copies.append(moved(source, target, sems, len(copies), c * step, step, part))
    copies.append(pltpu.make_async_copy(sd.at[used] if split else sd, s_down, sems.at[len(copies)]))
    for copy in copies:
        copy.start()
    outliers = cols.shape[1]
    for c in range(chunks):
        here = slice(c * step, (c + 1) * step)
        hot = jnp.where(iota((step, outliers), 0) + c * step == cols[...], 1.0, 0.0).astype(BF16)
        onehot[here, :] = hot
        count = lax.dot_general(
            jnp.ones((8, outliers), BF16), hot, (((1,), (1,)), ((), ())), preferred_element_type=F32
        )
        keep[:, here] = jnp.where(count == 0.0, 1.0, 0.0)
    for copy in copies:
        copy.wait()


def scaled(codes, scales, block):
    return jnp.concatenate(
        [
            codes[b * block : (b + 1) * block] * jnp.broadcast_to(scales[b : b + 1], (block, codes.shape[1]))
            for b in range(codes.shape[0] // block)
        ],
        axis=0,
    )


def expert_kernel(
    step, wide, count, gate, up, wd, onehot, keep, sg, su, sd, extra_gate, extra_up, *refs
):
    pieces, outs = refs[:count], refs[count : 2 * count]
    down, gate_acc, up_acc, picked, hidden_ref, gate_scale, up_scale, down_scale, sem = refs[2 * count :]
    height = pieces[0].shape[0]
    width, hid = gate.shape
    load = pltpu.make_async_copy(wd, down, sem)
    load.start()
    gate_acc[...] = jnp.zeros_like(gate_acc)
    up_acc[...] = jnp.zeros_like(up_acc)
    picked[...] = jnp.zeros_like(picked)
    gate_scale[...] = sg[...].astype(F32)
    up_scale[...] = su[...].astype(F32)
    down_scale[...] = sd[...].astype(F32)
    block = width // sg.shape[0]
    for c in range(width // step):
        here = slice(c * step, (c + 1) * step)
        there = slice(c * step // block, (c + 1) * step // block)
        whole = jnp.concatenate([piece[:, here] for piece in pieces], axis=0)
        masked = whole * jnp.broadcast_to(keep[0:1, here].astype(BF16), whole.shape)
        picked[...] += matmul(whole, onehot[here, :])
        gate_acc[...] += matmul(masked, scaled(gate[here, :], gate_scale[there, :].astype(BF16), block))
        up_acc[...] += matmul(masked, scaled(up[here, :], up_scale[there, :].astype(BF16), block))

    outliers = picked[...].astype(BF16)
    gate_val = gate_acc[...] + matmul(outliers, extra_gate[...])
    up_val = up_acc[...] + matmul(outliers, extra_up[...])
    hidden_ref[...] = (gate_val / (1.0 + jnp.exp(-gate_val)) * up_val).astype(BF16)
    load.wait()
    tall = hid // sd.shape[0]
    for c in range(width // wide):
        here = slice(c * wide, (c + 1) * wide)
        weights = jnp.concatenate(
            [
                down[b * tall : (b + 1) * tall, here]
                * jnp.broadcast_to(down_scale[b : b + 1, here].astype(BF16), (tall, wide))
                for b in range(hid // tall)
            ],
            axis=0,
        )
        result = matmul(hidden_ref[...], weights).astype(BF16)
        for n, out in enumerate(outs):
            out[:, here] = result[n * height : (n + 1) * height]


def shared_kernel(step, wide, group, split, gate, up, down, *refs):
    pieces, outs = refs[: 2 * group], refs[2 * group : 3 * group]
    rows_ref, gate_acc, up_acc, hidden_ref = refs[3 * group :]
    height = pieces[0].shape[0]
    rows_ref[...] = jnp.concatenate([p[...].astype(F32) for p in pieces], axis=0).astype(BF16)
    gate_acc[...] = jnp.zeros_like(gate_acc)
    up_acc[...] = jnp.zeros_like(up_acc)
    for c in range(gate.shape[0] // step):
        here = slice(c * step, (c + 1) * step)
        gate_acc[...] += matmul(rows_ref[:, here], gate[here, :])
        up_acc[...] += matmul(rows_ref[:, here], up[here, :])
    value = gate_acc[...]
    hidden = value / (1.0 + jnp.exp(-value)) * up_acc[...]
    if not split:
        hidden = jnp.where(iota(hidden.shape, 0) // height % 2 == 0, hidden, 0.0)
    hidden_ref[...] = hidden.astype(BF16)
    for c in range(down.shape[1] // wide):
        here = slice(c * wide, (c + 1) * wide)
        result = matmul(hidden_ref[...], down[:, here])
        for n, out in enumerate(outs):
            out[:, here] = result[2 * n * height : 2 * (n + 1) * height].astype(out.dtype)


def share_kernel(cap, masks, rows, ids_ref, home_ref, weights_ref, out):
    parts = TILE // cap
    codes = slot_codes(ids_ref, home_ref[0], rows, cap)
    weights = [weights_ref[t, r] for r in range(rows) for t in range(TOPK)]
    shape = (parts * rows, out.shape[1])
    i, j = iota(shape, 0), iota(shape, 1)
    code = block_codes(j // TILE, j % cap, cap, masks)
    same = j % TILE // cap == i // rows
    position = iota((parts * rows, 1), 0) % rows
    rest = jnp.zeros(shape, F32)
    for t in range(TOPK):
        rest += jnp.where(
            same & (code == by_row(codes, position, rows, t)),
            by_row(weights, position, rows, t),
            0.0,
        )
    for k in range(3):
        term = rest.astype(BF16)
        out[k * parts * rows : (k + 1) * parts * rows, :] = term
        rest = rest - term.astype(F32)


def combine_kernel(cap, count, first, start, share_ref, mine_ref, *refs):
    others, blocks, out = refs[:count], refs[count:-1], refs[-1]
    rows = out.shape[0]
    parts = TILE // cap
    width = out.shape[1] // parts
    arrived = jnp.concatenate([b[start : start + TILE, :] for b in blocks], axis=0)
    terms = matmul(share_ref[...], arrived)
    size = parts * rows
    routed = terms[:size] + terms[size : 2 * size] + terms[2 * size :]
    for q in range(parts):
        here = slice(q * width, (q + 1) * width)
        total = routed[q * rows : (q + 1) * rows]
        for other in (mine_ref,) + others:
            total += other[:, here].astype(F32)[first : first + rows]
        out[:, here] = total.astype(out.dtype)


def add_kernel(mine_ref, other_ref, out):
    out[...] = (mine_ref[...] + other_ref[...].astype(F32)).astype(out.dtype)


def on_device(
    tokens,
    expert_ids,
    gate_weights,
    w_gate,
    scale_gate,
    w_up,
    scale_up,
    w_down,
    scale_down,
    outlier_cols,
    outlier_gate,
    outlier_up,
    shared_gate,
    shared_up,
    shared_down,
):
    devices = lax.axis_size("ep")
    device = lax.axis_index("ep")
    hid = w_gate.shape[2]
    group = FF // hid
    experts = devices // group
    bits = group.bit_length() - 1
    rows, width = tokens.shape[1], tokens.shape[2]
    cap = max(2, rows * TOPK * 2 // experts)
    home = device // group
    part_width = width * cap // TILE
    slots = experts * cap

    def swap(array, mask):
        return lax.ppermute(array, "ep", [(d, d ^ mask) for d in range(devices)])

    def spread(pieces):
        for bit in range(bits):
            pieces = pieces + [swap(piece, 1 << bit) for piece in pieces]
        return pieces

    current = tokens[0]
    ids, weights = expert_ids[0].T, gate_weights[0].T
    home_ref = home.astype(jnp.int32).reshape(1)
    columns = experts // 2
    masks = [0] + sorted(range(2, experts, 2), key=lambda m: -m.bit_length())

    neighbour_ids, neighbour_weights = swap(ids, group), swap(weights, group)
    neighbour, own_rows = swap(current, group), spread([current])
    hit = pl.pallas_call(
        functools.partial(choose_kernel, cap, masks, rows),
        in_specs=[SMEM] * 3,
        out_specs=VMEM,
        out_shape=jax.ShapeDtypeStruct((columns * 2 * TILE, 2 * TILE // cap * rows), F32),
        compiler_params=params(4),
        cost_estimate=cost(1e6, 1e6),
        name="choose",
    )(ids, neighbour_ids, home_ref)
    hit, neighbour, neighbour_weights, own_rows = lax.optimization_barrier(
        (hit, neighbour, neighbour_weights, own_rows)
    )
    sent = pl.pallas_call(
        functools.partial(send_kernel, cap),
        in_specs=[VMEM, ANY, VMEM],
        out_specs=[VMEM] * columns,
        out_shape=[jax.ShapeDtypeStruct((2 * TILE, part_width), BF16)] * columns,
        scratch_shapes=[
            pltpu.VMEM((rows, width), BF16),
            pltpu.VMEM((2 * TILE // cap * rows, part_width), F32),
            pltpu.SemaphoreType.DMA,
        ],
        compiler_params=params(8),
        cost_estimate=cost(1e8, 1e6),
        name="send",
    )(hit, in_hbm(current), neighbour)

    def across(blocks):
        return [blocks[0]] + [swap(block, mask * group) for mask, block in zip(masks[1:], blocks[1:])]

    arrived = across(sent)
    cols, _ = lax.optimization_barrier((lax.dynamic_slice_in_dim(outlier_cols, home, 1, 0), sent[0]))
    step = 1024
    units = hid // 2 if hid % 256 == 0 else hid
    stored = jax.ShapeDtypeStruct((width, hid), BF16)
    gate, up, *shared_weights, onehot, keep = pl.pallas_call(
        functools.partial(load_kernel, step),
        in_specs=[SMEM] + [ANY] * 5 + [VMEM],
        out_specs=[VMEM] * 7,
        out_shape=[
            stored,
            stored,
            jax.ShapeDtypeStruct((width, units), BF16),
            jax.ShapeDtypeStruct((width, units), BF16),
            jax.ShapeDtypeStruct((units, width), BF16),
            jax.ShapeDtypeStruct((width, outlier_cols.shape[1]), BF16),
            jax.ShapeDtypeStruct((8, width), F32),
        ],
        scratch_shapes=[pltpu.SemaphoreType.DMA((4 * width // step + 1,))],
        compiler_params=params(8),
        cost_estimate=cost(1e9, 4 * hid * width),
        name="load",
    )(
        home_ref & 1,
        in_hbm(w_gate[0]),
        in_hbm(w_up[0]),
        in_hbm(shared_gate[0]),
        in_hbm(shared_up[0]),
        in_hbm(shared_down[0]),
        cols,
    )
    arrived, keep, neighbour = lax.optimization_barrier((arrived, keep, neighbour))
    row_pieces = [p for pair in zip(own_rows, spread([neighbour])) for p in pair]

    whole = jax.ShapeDtypeStruct((slots, width), BF16)
    taken = pl.pallas_call(
        functools.partial(unpack_kernel, cap),
        in_specs=[VMEM] * len(arrived),
        out_specs=VMEM,
        out_shape=whole,
        compiler_params=params(16),
        cost_estimate=cost(1e8, 1e6),
        name="unpack",
    )(*arrived)
    pieces = spread([taken])

    row_pieces, _ = lax.optimization_barrier((row_pieces, taken))
    shared = pl.pallas_call(
        functools.partial(shared_kernel, step, 1024, group, units < hid),
        in_specs=[VMEM] * (3 + 2 * group),
        out_specs=[VMEM] * group,
        out_shape=[jax.ShapeDtypeStruct((2 * rows, width), F32)]
        + [jax.ShapeDtypeStruct((2 * rows, width), BF16)] * (group - 1),
        scratch_shapes=[
            pltpu.VMEM((2 * group * rows, width), BF16),
            pltpu.VMEM((2 * group * rows, units), F32),
            pltpu.VMEM((2 * group * rows, units), F32),
            pltpu.VMEM((2 * group * rows, units), BF16),
        ],
        compiler_params=params(12),
        cost_estimate=cost(6 * group * rows * width * hid, 3 * hid * width),
        name="shared",
    )(*shared_weights, *row_pieces)
    pieces, first = lax.optimization_barrier((pieces, shared[0]))
    shared = [first] + list(shared[1:])
    others = [swap(shared[n], n) for n in range(1, group)]

    partials = pl.pallas_call(
        functools.partial(expert_kernel, step, 1024, group),
        in_specs=[VMEM, VMEM, ANY] + [VMEM] * (7 + group),
        out_specs=[VMEM] * group,
        out_shape=[whole] * group,
        scratch_shapes=[
            pltpu.VMEM((hid, width), BF16),
            pltpu.VMEM((group * slots, hid), F32),
            pltpu.VMEM((group * slots, hid), F32),
            pltpu.VMEM((group * slots, outlier_cols.shape[1]), F32),
            pltpu.VMEM((group * slots, hid), BF16),
            pltpu.VMEM(scale_gate.shape[1:], F32),
            pltpu.VMEM(scale_up.shape[1:], F32),
            pltpu.VMEM(scale_down.shape[1:], F32),
            pltpu.SemaphoreType.DMA,
        ],
        compiler_params=params(24),
        cost_estimate=cost(6 * group * slots * width * hid, 6 * hid * width),
        name="expert",
    )(
        gate,
        up,
        in_hbm(w_down[0]),
        onehot,
        keep,
        scale_gate[0],
        scale_up[0],
        scale_down[0],
        outlier_gate[0],
        outlier_up[0],
        *pieces,
    )

    for bit in reversed(range(1, bits)):
        half = 1 << bit
        partials = [
            (mine.astype(F32) + swap(other, half).astype(F32)).astype(BF16)
            for mine, other in zip(partials[:half], partials[half:])
        ]
    returning = pl.pallas_call(
        functools.partial(pack_kernel, cap),
        in_specs=[VMEM] * 2,
        out_specs=[VMEM] * columns,
        out_shape=[jax.ShapeDtypeStruct((2 * TILE, part_width), BF16)] * columns,
        compiler_params=params(16),
        cost_estimate=cost(1e8, 1e6),
        name="pack",
    )(partials[0], swap(partials[1], 1))
    returned = across(returning)

    def share(ids, weights):
        return pl.pallas_call(
            functools.partial(share_kernel, cap, masks, rows),
            in_specs=[SMEM] * 3,
            out_specs=VMEM,
            out_shape=jax.ShapeDtypeStruct((3 * TILE // cap * rows, columns * TILE), BF16),
            compiler_params=params(4),
            cost_estimate=cost(1e6, 1e5),
            name="share",
        )(ids, home_ref, weights)

    def combine(own, shares):
        return pl.pallas_call(
            functools.partial(
                combine_kernel, cap, group - 1, 0 if own else rows, 0 if own else TILE
            ),
            in_specs=[VMEM] * (1 + group + columns),
            out_specs=VMEM,
            out_shape=jax.ShapeDtypeStruct((rows, width), F32 if own else BF16),
            compiler_params=params(16),
            cost_estimate=cost(1e8, 1e6),
            name="combine",
        )(shares, shared[0], *others, *returned)

    shares = [share(neighbour_ids, neighbour_weights), share(ids, weights)]
    shares, others = lax.optimization_barrier((shares, others))
    crossing = combine(False, shares[0])
    mine, crossing = lax.optimization_barrier((shares[1], crossing))
    mine = combine(True, mine)
    out = pl.pallas_call(
        add_kernel,
        in_specs=[VMEM] * 2,
        out_specs=VMEM,
        out_shape=jax.ShapeDtypeStruct((rows, width), BF16),
        compiler_params=params(4),
        cost_estimate=cost(1e6, 1e6),
        name="add",
    )(mine, swap(crossing, group))
    return out[None]


def solution(mesh):
    rows = P(None, ("parts", "ep"), None)
    held = P("ep", None, None)
    placed = (rows, rows, rows) + (held,) * 6 + (P(),) + (held,) * 5
    return jax.shard_map(
        on_device, mesh=mesh, in_specs=placed, out_specs=rows, check_vma=False
    )
```

```python
import functools

import jax
import jax.numpy as jnp
from jax import lax
from jax.experimental import pallas as pl
from jax.experimental.pallas import tpu as pltpu
from jax.sharding import PartitionSpec as P

FF = 1024
TOPK = 2
TILE = 16
LANES = 128
BF16 = jnp.bfloat16
F32 = jnp.float32
VMEM = pl.BlockSpec(memory_space=pltpu.VMEM)
ANY = pl.BlockSpec(memory_space=pl.ANY)
SMEM = pl.BlockSpec(memory_space=pltpu.SMEM)


def params(mib):
    return pltpu.CompilerParams(vmem_limit_bytes=mib << 20)


def cost(flops, nbytes):
    return pl.CostEstimate(flops=int(flops), bytes_accessed=int(nbytes), transcendentals=0)


def matmul(left, right):
    return jnp.dot(left, right, preferred_element_type=F32)


def in_hbm(array):
    return pltpu.with_memory_space_constraint(array, pltpu.HBM)


def iota(shape, dim):
    return lax.broadcasted_iota(jnp.int32, shape, dim)


def by_row(values, position, choice):
    out = jnp.zeros(position.shape, values[0].dtype)
    for r in range(len(values) // TOPK):
        out = jnp.where(position == r, values[r * TOPK + choice], out)
    return out


def slot_marks(ids_ref, weights_ref, home, rows, cap):
    pairs = [(r, t) for r in range(rows) for t in range(TOPK)]
    ids = [ids_ref[t, r] for r, t in pairs]
    weights = [weights_ref[t, r] for r, t in pairs]
    own, other = [], []
    for n, e in enumerate(ids):
        place = jnp.int32(0)
        for earlier in ids[:n]:
            place += (earlier == e).astype(jnp.int32)
        apart = e ^ home
        code = (apart >> 1) * cap + place
        own.append(jnp.where(apart & 1 == 0, code, -1))
        other.append(jnp.where(apart & 1 == 1, code, -1))
    shape = (rows, LANES)
    position, lane = iota(shape, 0), iota(shape, 1)
    quarter = LANES // 4
    marks = [jnp.zeros(shape, F32), jnp.zeros(shape, F32)]
    for t in range(TOPK):
        rest = by_row(weights, position, t)
        value = jnp.ones(shape, F32)
        for k in range(1, 4):
            term = rest.astype(BF16).astype(F32)
            value = jnp.where(lane // quarter == k, term, value)
            rest = rest - term
        for n, codes in enumerate((own, other)):
            marks[n] += jnp.where(lane % quarter == by_row(codes, position, t), value, 0.0)
    return marks


def block_lanes(shape, dim, cap, masks):
    j = iota(shape, dim)
    lane = j % cap
    for n, mask in enumerate(masks):
        lane += jnp.where(j // TILE == n, mask // 2 * cap, 0)
    return lane, j % TILE // cap


def tiled(marks, cap):
    return jnp.concatenate([marks.astype(F32)] * (TILE // cap), axis=0).astype(BF16)


def lanes_dot(left, right):
    return lax.dot_general(left, right, (((1,), (1,)), ((), ())), preferred_element_type=F32)


def write_blocks(cap, masks, marks, tokens, stacked, blocks):
    rows = marks.shape[0]
    parts = TILE // cap
    width = blocks[0].shape[1]
    height = len(blocks) * TILE
    lane, part = block_lanes((height, LANES), 0, cap, masks)
    wanted = jnp.where(lane == iota((height, LANES), 1), 1.0, 0.0).astype(BF16)
    hit = lanes_dot(wanted, tiled(marks, cap))
    part = block_lanes(hit.shape, 0, cap, masks)[1]
    hit = jnp.where(part == iota(hit.shape, 1) // rows, hit, 0.0)
    for q in range(parts):
        stacked[q * rows : (q + 1) * rows, :] = tokens[:, q * width : (q + 1) * width].astype(F32)
    chosen = matmul(hit.astype(BF16), stacked[...].astype(BF16)).astype(BF16)
    for m, block in enumerate(blocks):
        block[...] = chosen[m * TILE : (m + 1) * TILE]


def first_kernel(cap, masks, home_ref, ids_hbm, weights_hbm, own_hbm, other_ref, marks_ref, *refs):
    blocks, (ids_ref, weights_ref, own, stacked, sems) = refs[:-5], refs[-5:]
    small = [
        pltpu.make_async_copy(ids_hbm, ids_ref, sems.at[1]),
        pltpu.make_async_copy(weights_hbm, weights_ref, sems.at[2]),
    ]
    copy = pltpu.make_async_copy(own_hbm, own, sems.at[0])
    for each in small:
        each.start()
    copy.start()
    for each in small:
        each.wait()
    rows = own.shape[0]
    marks, other = slot_marks(ids_ref, weights_ref, home_ref[0], rows, cap)
    marks_ref[...] = marks.astype(BF16)
    other_ref[...] = other.astype(BF16)
    copy.wait()
    write_blocks(cap, masks, marks, own, stacked, blocks)


def send_kernel(cap, masks, marks, tokens, *refs):
    count = len(masks)
    own, blocks, stacked = refs[:count], refs[count : 2 * count], refs[2 * count]
    for mine, block in zip(own, blocks):
        block[:TILE, :] = mine[...]
    lower = [block.at[pl.ds(TILE, TILE)] for block in blocks]
    write_blocks(cap, masks, marks[...], tokens, stacked, lower)


def unpack_kernel(cap, *refs):
    blocks, out = refs[:-1], refs[-1]
    parts, slots, width = TILE // cap, out.shape[0], blocks[0].shape[1]
    shape = (parts * slots, slots // cap * TILE)
    i, j = iota(shape, 0), iota(shape, 1)
    source = i % slots // cap * TILE + i // slots * cap + i % cap
    arranged = matmul(
        jnp.where(source == j, 1.0, 0.0).astype(BF16),
        jnp.concatenate([b[...] for b in blocks], axis=0),
    ).astype(BF16)
    for q in range(parts):
        out[:, q * width : (q + 1) * width] = arranged[q * slots : (q + 1) * slots]


def pack_kernel(cap, mine_ref, other_ref, *blocks):
    parts, slots = TILE // cap, mine_ref.shape[0]
    width = mine_ref.shape[1] // parts
    total = (mine_ref[...].astype(F32) + other_ref[...].astype(F32)).astype(BF16)
    shape = (slots // cap * TILE, parts * slots)
    j, i = iota(shape, 0), iota(shape, 1)
    source = j % TILE // cap * slots + j // TILE * cap + j % cap
    arranged = matmul(
        jnp.where(source == i, 1.0, 0.0).astype(BF16),
        jnp.concatenate([total[:, q * width : (q + 1) * width] for q in range(parts)], axis=0),
    ).astype(BF16)
    start = 0
    for block in blocks:
        block[...] = arranged[start : start + block.shape[0]]
        start += block.shape[0]


def moved(source, target, sems, k, start, size, units=None):
    here = pl.ds(start, size)
    source = source.at[here] if units is None else source.at[here, units]
    return pltpu.make_async_copy(source, target.at[here], sems.at[k])


def load_kernel(step, wg, wu, cols, gate, up, onehot, keep, sems):
    chunks = wg.shape[0] // step
    copies = [
        moved(source, target, sems, 2 * c + k, c * step, step)
        for c in range(chunks)
        for k, (source, target) in enumerate(((wg, gate), (wu, up)))
    ]
    for copy in copies:
        copy.start()
    outliers = cols.shape[1]
    for c in range(chunks):
        here = slice(c * step, (c + 1) * step)
        hot = jnp.where(iota((step, outliers), 0) + c * step == cols[...], 1.0, 0.0).astype(BF16)
        onehot[here, :] = hot
        count = lanes_dot(jnp.ones((8, outliers), BF16), hot)
        keep[:, here] = jnp.where(count == 0.0, 1.0, 0.0)
    for copy in copies:
        copy.wait()


def scaled(codes, scales, block):
    return jnp.concatenate(
        [
            codes[b * block : (b + 1) * block] * jnp.broadcast_to(scales[b : b + 1], (block, codes.shape[1]))
            for b in range(codes.shape[0] // block)
        ],
        axis=0,
    )


def expert_kernel(
    step, wide, count, gate, up, wd, onehot, keep, sg, su, sd, extra_gate, extra_up, *refs
):
    pieces, outs = refs[:count], refs[count : 2 * count]
    down, gate_acc, up_acc, picked, hidden_ref, gate_scale, up_scale, down_scale, sem = refs[2 * count :]
    height = pieces[0].shape[0]
    width, hid = gate.shape
    chunks = width // step
    load = pltpu.make_async_copy(wd, down, sem)
    load.start()
    gate_acc[...] = jnp.zeros_like(gate_acc)
    up_acc[...] = jnp.zeros_like(up_acc)
    picked[...] = jnp.zeros_like(picked)
    gate_scale[...] = sg[...].astype(F32)
    up_scale[...] = su[...].astype(F32)
    down_scale[...] = sd[...].astype(F32)
    block = width // sg.shape[0]
    for c in range(chunks):
        here = slice(c * step, (c + 1) * step)
        there = slice(c * step // block, (c + 1) * step // block)
        whole = jnp.concatenate([piece[:, here] for piece in pieces], axis=0)
        masked = whole * jnp.broadcast_to(keep[0:1, here].astype(BF16), whole.shape)
        picked[...] += matmul(whole, onehot[here, :])
        gate_acc[...] += matmul(masked, scaled(gate[here, :], gate_scale[there, :].astype(BF16), block))
        up_acc[...] += matmul(masked, scaled(up[here, :], up_scale[there, :].astype(BF16), block))

    outliers = picked[...].astype(BF16)
    gate_val = gate_acc[...] + matmul(outliers, extra_gate[...])
    up_val = up_acc[...] + matmul(outliers, extra_up[...])
    hidden_ref[...] = (gate_val / (1.0 + jnp.exp(-gate_val)) * up_val).astype(BF16)
    load.wait()
    tall = hid // sd.shape[0]
    for c in range(width // wide):
        here = slice(c * wide, (c + 1) * wide)
        weights = jnp.concatenate(
            [
                down[b * tall : (b + 1) * tall, here]
                * jnp.broadcast_to(down_scale[b : b + 1, here].astype(BF16), (tall, wide))
                for b in range(hid // tall)
            ],
            axis=0,
        )
        result = matmul(hidden_ref[...], weights).astype(BF16)
        for n, out in enumerate(outs):
            out[:, here] = result[n * height : (n + 1) * height]


def shared_kernel(step, wide, group, half_ref, wg, wu, wd, *refs):
    pieces, outs = refs[: 2 * group], refs[2 * group : 4 * group]
    gate, up, down, rows_ref, gate_acc, up_acc, hidden_ref, sems = refs[4 * group :]
    height = pieces[0].shape[0]
    width, units = gate.shape
    chunks = width // step
    split = units < wg.shape[1]
    used = pl.ds(pl.multiple_of(half_ref[0] * units, units), units) if split else None
    copies = []
    for c in range(chunks):
        for source, target in ((wg, gate), (wu, up)):
            copies.append(moved(source, target, sems, len(copies), c * step, step, used))
    copies.append(pltpu.make_async_copy(wd.at[used] if split else wd, down, sems.at[len(copies)]))
    for copy in copies:
        copy.start()
    rows_ref[...] = jnp.concatenate([p[:, :width].astype(F32) for p in pieces], axis=0).astype(BF16)
    gate_acc[...] = jnp.zeros_like(gate_acc)
    up_acc[...] = jnp.zeros_like(up_acc)
    for c in range(chunks):
        here = slice(c * step, (c + 1) * step)
        copies[2 * c].wait()
        gate_acc[...] += matmul(rows_ref[:, here], gate[here, :])
        copies[2 * c + 1].wait()
        up_acc[...] += matmul(rows_ref[:, here], up[here, :])
    value = gate_acc[...]
    hidden = value / (1.0 + jnp.exp(-value)) * up_acc[...]
    if not split:
        hidden = jnp.where(iota(hidden.shape, 0) // height % 2 == 0, hidden, 0.0)
    hidden_ref[...] = hidden.astype(BF16)
    copies[-1].wait()
    for c in range(width // wide):
        here = slice(c * wide, (c + 1) * wide)
        result = matmul(hidden_ref[...], down[:, here])
        for n, out in enumerate(outs):
            out[:, here] = result[n * height : (n + 1) * height].astype(out.dtype)


def share_kernel(cap, masks, *refs):
    for marks, out in zip(refs[: len(refs) // 2], refs[len(refs) // 2 :]):
        rows = marks.shape[0]
        size, height = TILE // cap * rows, out.shape[1]
        repeated = tiled(marks[...], cap)
        lane, _ = block_lanes((height, LANES), 0, cap, masks)
        part = block_lanes((size, height), 1, cap, masks)[1]
        same = part == iota((size, height), 0) // rows
        for k in range(3):
            wanted = lane + (k + 1) * (LANES // 4) == iota((height, LANES), 1)
            term = lanes_dot(repeated, jnp.where(wanted, 1.0, 0.0).astype(BF16))
            out[k * size : (k + 1) * size, :] = jnp.where(same, term, 0.0).astype(BF16)


def combine_kernel(cap, start, share_ref, *refs):
    blocks, out = refs[:-1], refs[-1]
    rows = out.shape[0]
    parts = TILE // cap
    width = out.shape[1] // parts
    arrived = jnp.concatenate([b[start : start + TILE, :] for b in blocks], axis=0)
    terms = matmul(share_ref[...], arrived)
    size = parts * rows
    routed = terms[:size] + terms[size : 2 * size] + terms[2 * size :]
    for q in range(parts):
        out[:, q * width : (q + 1) * width] = routed[q * rows : (q + 1) * rows]


def merge_kernel(routed, *refs):
    out = refs[-1]
    total = routed[...]
    for part in refs[:-1]:
        total += part[...].astype(F32)
    out[...] = total.astype(out.dtype)


def add_kernel(mine_ref, other_ref, out):
    out[...] = (mine_ref[...] + other_ref[...].astype(F32)).astype(out.dtype)


def on_device(
    tokens,
    expert_ids,
    gate_weights,
    w_gate,
    scale_gate,
    w_up,
    scale_up,
    w_down,
    scale_down,
    outlier_cols,
    outlier_gate,
    outlier_up,
    shared_gate,
    shared_up,
    shared_down,
):
    devices = lax.axis_size("ep")
    device = lax.axis_index("ep")
    hid = w_gate.shape[2]
    group = FF // hid
    experts = devices // group
    bits = group.bit_length() - 1
    rows, width = tokens.shape[1], tokens.shape[2]
    cap = max(2, rows * TOPK * 2 // experts)
    home = device // group
    part_width = width * cap // TILE
    slots = experts * cap

    def swap(array, mask):
        return lax.ppermute(array, "ep", [(d, d ^ mask) for d in range(devices)])

    def spread(pieces):
        for bit in range(bits):
            pieces = pieces + [swap(piece, 1 << bit) for piece in pieces]
        return pieces

    current = tokens[0]
    ids, weights = expert_ids[0].T, gate_weights[0].T
    home_ref = home.astype(jnp.int32).reshape(1)
    columns = experts // 2
    masks = [0] + sorted(range(2, experts, 2), key=lambda m: -m.bit_length())

    parts = TILE // cap
    sent_block = jax.ShapeDtypeStruct((TILE, part_width), BF16)
    stack = pltpu.VMEM((parts * rows, part_width), F32)
    marks_to_send, marks, *own_blocks = pl.pallas_call(
        functools.partial(first_kernel, cap, masks),
        in_specs=[SMEM] + [ANY] * 3,
        out_specs=[VMEM] * (2 + columns),
        out_shape=[
            jax.ShapeDtypeStruct((rows, LANES), BF16),
            jax.ShapeDtypeStruct((rows, LANES), BF16),
        ]
        + [sent_block] * columns,
        scratch_shapes=[
            pltpu.SMEM(ids.shape, jnp.int32),
            pltpu.SMEM(weights.shape, F32),
            pltpu.VMEM((rows, width), BF16),
            stack,
            pltpu.SemaphoreType.DMA((3,)),
        ],
        compiler_params=params(8),
        cost_estimate=cost(1e8, 1e6),
        name="first",
    )(home_ref, in_hbm(ids), in_hbm(weights), in_hbm(current))
    def across(blocks):
        return [blocks[0]] + [swap(block, mask * group) for mask, block in zip(masks[1:], blocks[1:])]

    neighbour, neighbour_marks = swap(current, group), swap(marks_to_send, group)
    blocks = pl.pallas_call(
        functools.partial(send_kernel, cap, masks),
        in_specs=[VMEM] * (2 + columns),
        out_specs=[VMEM] * columns,
        out_shape=[jax.ShapeDtypeStruct((2 * TILE, part_width), BF16)] * columns,
        scratch_shapes=[stack],
        compiler_params=params(8),
        cost_estimate=cost(1e8, 1e6),
        name="send",
    )(neighbour_marks, neighbour, *own_blocks)
    arrived = across(blocks)

    cols, _ = lax.optimization_barrier((lax.dynamic_slice_in_dim(outlier_cols, home, 1, 0), blocks[0]))
    step = 1024
    units = hid // 2 if hid % 256 == 0 else hid
    gate, up, onehot, keep = pl.pallas_call(
        functools.partial(load_kernel, step),
        in_specs=[ANY, ANY, VMEM],
        out_specs=[VMEM] * 4,
        out_shape=[
            jax.ShapeDtypeStruct((width, hid), BF16),
            jax.ShapeDtypeStruct((width, hid), BF16),
            jax.ShapeDtypeStruct((width, outlier_cols.shape[1]), BF16),
            jax.ShapeDtypeStruct((8, width), F32),
        ],
        scratch_shapes=[pltpu.SemaphoreType.DMA((2 * width // step,))],
        compiler_params=params(8),
        cost_estimate=cost(1e9, 2 * hid * width),
        name="load",
    )(in_hbm(w_gate[0]), in_hbm(w_up[0]), cols)
    arrived, keep = lax.optimization_barrier((arrived, keep))

    whole = jax.ShapeDtypeStruct((slots, width), BF16)
    taken = pl.pallas_call(
        functools.partial(unpack_kernel, cap),
        in_specs=[VMEM] * len(arrived),
        out_specs=VMEM,
        out_shape=whole,
        compiler_params=params(16),
        cost_estimate=cost(1e8, 1e6),
        name="unpack",
    )(*arrived)
    pieces = spread([taken])

    neighbour_marks, _ = lax.optimization_barrier((neighbour_marks, taken))
    back = list(range(columns))
    shares = pl.pallas_call(
        functools.partial(share_kernel, cap, [masks[n] for n in back]),
        in_specs=[VMEM] * 2,
        out_specs=[VMEM] * 2,
        out_shape=[jax.ShapeDtypeStruct((3 * parts * rows, columns * TILE), BF16)] * 2,
        compiler_params=params(4),
        cost_estimate=cost(1e6, 1e5),
        name="share",
    )(neighbour_marks, marks)
    pieces, shares = lax.optimization_barrier((pieces, shares))

    partials = pl.pallas_call(
        functools.partial(expert_kernel, step, 1024, group),
        in_specs=[VMEM, VMEM, ANY] + [VMEM] * (7 + group),
        out_specs=[VMEM] * group,
        out_shape=[whole] * group,
        scratch_shapes=[
            pltpu.VMEM((hid, width), BF16),
            pltpu.VMEM((group * slots, hid), F32),
            pltpu.VMEM((group * slots, hid), F32),
            pltpu.VMEM((group * slots, outlier_cols.shape[1]), F32),
            pltpu.VMEM((group * slots, hid), BF16),
            pltpu.VMEM(scale_gate.shape[1:], F32),
            pltpu.VMEM(scale_up.shape[1:], F32),
            pltpu.VMEM(scale_down.shape[1:], F32),
            pltpu.SemaphoreType.DMA,
        ],
        compiler_params=params(24),
        cost_estimate=cost(6 * group * slots * width * hid, 6 * hid * width),
        name="expert",
    )(
        gate,
        up,
        in_hbm(w_down[0]),
        onehot,
        keep,
        scale_gate[0],
        scale_up[0],
        scale_down[0],
        outlier_gate[0],
        outlier_up[0],
        *pieces,
    )

    for bit in reversed(range(1, bits)):
        half = 1 << bit
        partials = [
            (mine.astype(F32) + swap(other, half).astype(F32)).astype(BF16)
            for mine, other in zip(partials[:half], partials[half:])
        ]
    returning = pl.pallas_call(
        functools.partial(pack_kernel, cap),
        in_specs=[VMEM] * 2,
        out_specs=[VMEM] * columns,
        out_shape=[jax.ShapeDtypeStruct((2 * TILE, part_width), BF16)] * columns,
        compiler_params=params(16),
        cost_estimate=cost(1e8, 1e6),
        name="pack",
    )(partials[0], swap(partials[1], 1))
    returned = [across(returning)[n] for n in back]

    row_pieces = [p for pair in zip(spread([current]), spread([neighbour])) for p in pair]
    row_pieces, _ = lax.optimization_barrier((row_pieces, returning[0]))
    shared = pl.pallas_call(
        functools.partial(shared_kernel, step, 1024, group),
        in_specs=[SMEM] + [ANY] * 3 + [VMEM] * (2 * group),
        out_specs=[VMEM] * (2 * group),
        out_shape=[jax.ShapeDtypeStruct((rows, width), F32)] * 2
        + [jax.ShapeDtypeStruct((rows, width), BF16)] * (2 * group - 2),
        scratch_shapes=[
            pltpu.VMEM((width, units), BF16),
            pltpu.VMEM((width, units), BF16),
            pltpu.VMEM((units, width), BF16),
            pltpu.VMEM((2 * group * rows, width), BF16),
            pltpu.VMEM((2 * group * rows, units), F32),
            pltpu.VMEM((2 * group * rows, units), F32),
            pltpu.VMEM((2 * group * rows, units), BF16),
            pltpu.SemaphoreType.DMA((2 * width // step + 1,)),
        ],
        compiler_params=params(24),
        cost_estimate=cost(6 * group * rows * width * hid, 3 * hid * width),
        name="shared",
    )(
        home_ref & 1,
        in_hbm(shared_gate[0]),
        in_hbm(shared_up[0]),
        in_hbm(shared_down[0]),
        *row_pieces,
    )
    shared_sums = [[shared[k]] + [swap(shared[2 * n + k], n) for n in range(1, group)] for k in (0, 1)]
    def combine(own, shares):
        return pl.pallas_call(
            functools.partial(combine_kernel, cap, 0 if own else TILE),
            in_specs=[VMEM] * (1 + columns),
            out_specs=VMEM,
            out_shape=jax.ShapeDtypeStruct((rows, width), F32),
            compiler_params=params(16),
            cost_estimate=cost(1e8, 1e6),
            name="combine",
        )(shares, *returned)

    def merge(own, routed):
        return pl.pallas_call(
            merge_kernel,
            in_specs=[VMEM] * (1 + group),
            out_specs=VMEM,
            out_shape=jax.ShapeDtypeStruct((rows, width), F32 if own else BF16),
            compiler_params=params(8),
            cost_estimate=cost(1e6, 1e6),
            name="merge",
        )(routed, *shared_sums[0 if own else 1])

    crossing = combine(False, shares[0])
    shared_sums[1], crossing = lax.optimization_barrier((shared_sums[1], crossing))
    crossing = merge(False, crossing)
    mine, crossing = lax.optimization_barrier((shares[1], crossing))
    mine = merge(True, combine(True, mine))
    out = pl.pallas_call(
        add_kernel,
        in_specs=[VMEM] * 2,
        out_specs=VMEM,
        out_shape=jax.ShapeDtypeStruct((rows, width), BF16),
        compiler_params=params(4),
        cost_estimate=cost(1e6, 1e6),
        name="add",
    )(mine, swap(crossing, group))
    return out[None]


def solution(mesh):
    rows = P(None, ("parts", "ep"), None)
    held = P("ep", None, None)
    placed = (rows, rows, rows) + (held,) * 6 + (P(),) + (held,) * 5
    return jax.shard_map(
        on_device, mesh=mesh, in_specs=placed, out_specs=rows, check_vma=False
    )
```

```python
import functools

import jax
import jax.numpy as jnp
from jax import lax
from jax.experimental import pallas as pl
from jax.experimental.pallas import tpu as pltpu
from jax.sharding import PartitionSpec as P

FF = 1024
TOPK = 2
TILE = 16
LANES = 128
AHEAD = 2e11
BF16 = jnp.bfloat16
F32 = jnp.float32
VMEM = pl.BlockSpec(memory_space=pltpu.VMEM)
ANY = pl.BlockSpec(memory_space=pl.ANY)
SMEM = pl.BlockSpec(memory_space=pltpu.SMEM)


def params(mib):
    return pltpu.CompilerParams(vmem_limit_bytes=mib << 20)


def cost(flops, nbytes):
    return pl.CostEstimate(flops=int(flops), bytes_accessed=int(nbytes), transcendentals=0)


def matmul(left, right):
    return jnp.dot(left, right, preferred_element_type=F32)


def in_hbm(array):
    return pltpu.with_memory_space_constraint(array, pltpu.HBM)


def iota(shape, dim):
    return lax.broadcasted_iota(jnp.int32, shape, dim)


def by_row(values, position, choice):
    out = jnp.zeros(position.shape, values[0].dtype)
    for r in range(len(values) // TOPK):
        out = jnp.where(position == r, values[r * TOPK + choice], out)
    return out


def slot_marks(ids_ref, weights_ref, rows, cap):
    pairs = [(r, t) for r in range(rows) for t in range(TOPK)]
    ids = [ids_ref[t, r] for r, t in pairs]
    weights = [weights_ref[t, r] for r, t in pairs]
    codes = []
    for n, e in enumerate(ids):
        place = jnp.int32(0)
        for earlier in ids[:n]:
            place += (earlier == e).astype(jnp.int32)
        codes.append(e * cap + place)
    shape = (rows, LANES)
    position, lane = iota(shape, 0), iota(shape, 1)
    quarter = LANES // 4
    marks = jnp.zeros(shape, F32)
    for t in range(TOPK):
        rest = by_row(weights, position, t)
        value = jnp.ones(shape, F32)
        for k in range(1, 4):
            term = rest.astype(BF16).astype(F32)
            value = jnp.where(lane // quarter == k, term, value)
            rest = rest - term
        marks += jnp.where(lane % quarter == by_row(codes, position, t), value, 0.0)
    return marks


def block_lanes(shape, dim, cap, masks, home):
    j = iota(shape, dim)
    lane = j % cap
    for n, mask in enumerate(masks):
        lane += jnp.where(j // TILE == n, (home ^ mask) * cap, 0)
    return lane, j % TILE // cap


def tiled(marks, cap):
    return jnp.concatenate([marks.astype(F32)] * (TILE // cap), axis=0).astype(BF16)


def lanes_dot(left, right):
    return lax.dot_general(left, right, (((1,), (1,)), ((), ())), preferred_element_type=F32)


def write_blocks(cap, masks, home, marks, tokens, stacked, blocks):
    rows = marks.shape[0]
    parts = TILE // cap
    width = blocks[0].shape[1]
    height = len(blocks) * TILE
    lane, _ = block_lanes((height, LANES), 0, cap, masks, home)
    wanted = jnp.where(lane == iota((height, LANES), 1), 1.0, 0.0).astype(BF16)
    hit = lanes_dot(wanted, tiled(marks, cap))
    part = iota(hit.shape, 0) % TILE // cap
    hit = jnp.where(part == iota(hit.shape, 1) // rows, hit, 0.0)
    for q in range(parts):
        stacked[q * rows : (q + 1) * rows, :] = tokens[:, q * width : (q + 1) * width].astype(F32)
    chosen = matmul(hit.astype(BF16), stacked[...].astype(BF16)).astype(BF16)
    for m, block in enumerate(blocks):
        block[...] = chosen[m * TILE : (m + 1) * TILE]


def first_kernel(cap, masks, home_ref, ids_hbm, weights_hbm, own_hbm, marks_ref, *refs):
    blocks, (ids_ref, weights_ref, own, stacked, sems) = refs[:-5], refs[-5:]
    small = [
        pltpu.make_async_copy(ids_hbm, ids_ref, sems.at[1]),
        pltpu.make_async_copy(weights_hbm, weights_ref, sems.at[2]),
    ]
    copy = pltpu.make_async_copy(own_hbm, own, sems.at[0])
    for each in small:
        each.start()
    copy.start()
    for each in small:
        each.wait()
    rows = own.shape[0]
    marks = slot_marks(ids_ref, weights_ref, rows, cap)
    marks_ref[...] = marks.astype(BF16)
    copy.wait()
    write_blocks(cap, masks, home_ref[0], marks, own, stacked, blocks)


def unpack_kernel(cap, *refs):
    blocks, out = refs[:-1], refs[-1]
    parts, slots, width = TILE // cap, out.shape[0], blocks[0].shape[1]
    shape = (parts * slots, slots // cap * TILE)
    i, j = iota(shape, 0), iota(shape, 1)
    source = i % slots // cap * TILE + i // slots * cap + i % cap
    arranged = matmul(
        jnp.where(source == j, 1.0, 0.0).astype(BF16),
        jnp.concatenate([b[...] for b in blocks], axis=0),
    ).astype(BF16)
    for q in range(parts):
        out[:, q * width : (q + 1) * width] = arranged[q * slots : (q + 1) * slots]


def pack_kernel(cap, mine_ref, other_ref, *blocks):
    parts, slots = TILE // cap, mine_ref.shape[0]
    width = mine_ref.shape[1] // parts
    total = (mine_ref[...].astype(F32) + other_ref[...].astype(F32)).astype(BF16)
    shape = (slots // cap * TILE, parts * slots)
    j, i = iota(shape, 0), iota(shape, 1)
    source = j % TILE // cap * slots + j // TILE * cap + j % cap
    arranged = matmul(
        jnp.where(source == i, 1.0, 0.0).astype(BF16),
        jnp.concatenate([total[:, q * width : (q + 1) * width] for q in range(parts)], axis=0),
    ).astype(BF16)
    start = 0
    for block in blocks:
        block[...] = arranged[start : start + block.shape[0]]
        start += block.shape[0]


def outlier_kernel(step, cols, *refs):
    onehot, keep = refs[-2:]
    chunks = onehot.shape[0] // step
    outliers = cols.shape[1]
    for c in range(chunks):
        here = slice(c * step, (c + 1) * step)
        hot = jnp.where(iota((step, outliers), 0) + c * step == cols[...], 1.0, 0.0).astype(BF16)
        onehot[here, :] = hot
        count = lanes_dot(jnp.ones((8, outliers), BF16), hot)
        keep[:, here] = jnp.where(count == 0.0, 1.0, 0.0)


def scaled(codes, scales, block):
    return jnp.concatenate(
        [
            codes[b * block : (b + 1) * block] * jnp.broadcast_to(scales[b : b + 1], (block, codes.shape[1]))
            for b in range(codes.shape[0] // block)
        ],
        axis=0,
    )


def expert_kernel(
    step, wide, count, gate, up, wd, onehot, keep, sg, su, sd, extra_gate, extra_up, *refs
):
    pieces, outs = refs[:count], refs[count : 2 * count]
    down, gate_acc, up_acc, picked, hidden_ref, gate_scale, up_scale, down_scale, sem = refs[2 * count :]
    height = pieces[0].shape[0]
    width, hid = gate.shape
    chunks = width // step
    load = pltpu.make_async_copy(wd, down, sem)
    load.start()
    gate_acc[...] = jnp.zeros_like(gate_acc)
    up_acc[...] = jnp.zeros_like(up_acc)
    picked[...] = jnp.zeros_like(picked)
    gate_scale[...] = sg[...].astype(F32)
    up_scale[...] = su[...].astype(F32)
    down_scale[...] = sd[...].astype(F32)
    block = width // sg.shape[0]
    for c in range(chunks):
        here = slice(c * step, (c + 1) * step)
        there = slice(c * step // block, (c + 1) * step // block)
        whole = jnp.concatenate([piece[:, here] for piece in pieces], axis=0)
        masked = whole * jnp.broadcast_to(keep[0:1, here].astype(BF16), whole.shape)
        picked[...] += matmul(whole, onehot[here, :])
        gate_acc[...] += matmul(masked, scaled(gate[here, :], gate_scale[there, :].astype(BF16), block))
        up_acc[...] += matmul(masked, scaled(up[here, :], up_scale[there, :].astype(BF16), block))

    outliers = picked[...].astype(BF16)
    gate_val = gate_acc[...] + matmul(outliers, extra_gate[...])
    up_val = up_acc[...] + matmul(outliers, extra_up[...])
    hidden_ref[...] = (gate_val / (1.0 + jnp.exp(-gate_val)) * up_val).astype(BF16)
    load.wait()
    tall = hid // sd.shape[0]
    for c in range(width // wide):
        here = slice(c * wide, (c + 1) * wide)
        weights = jnp.concatenate(
            [
                down[b * tall : (b + 1) * tall, here]
                * jnp.broadcast_to(down_scale[b : b + 1, here].astype(BF16), (tall, wide))
                for b in range(hid // tall)
            ],
            axis=0,
        )
        result = matmul(hidden_ref[...], weights).astype(BF16)
        for n, out in enumerate(outs):
            out[:, here] = result[n * height : (n + 1) * height]


def shared_up_kernel(step, gate, up, *refs):
    pieces, (hidden, rows_ref, gate_acc, up_acc) = refs[:-4], refs[-4:]
    rows_ref[...] = jnp.concatenate([p[...].astype(F32) for p in pieces], axis=0).astype(BF16)
    gate_acc[...] = jnp.zeros_like(gate_acc)
    up_acc[...] = jnp.zeros_like(up_acc)
    for c in range(gate.shape[0] // step):
        here = slice(c * step, (c + 1) * step)
        gate_acc[...] += matmul(rows_ref[:, here], gate[here, :])
        up_acc[...] += matmul(rows_ref[:, here], up[here, :])
    value = gate_acc[...]
    hidden[...] = (value / (1.0 + jnp.exp(-value)) * up_acc[...]).astype(BF16)


def shared_down_kernel(wide, hidden, down, *outs):
    height = outs[0].shape[0]
    for c in range(down.shape[1] // wide):
        here = slice(c * wide, (c + 1) * wide)
        result = matmul(hidden[...], down[:, here])
        for n, out in enumerate(outs):
            out[:, here] = result[n * height : (n + 1) * height].astype(out.dtype)


def share_kernel(cap, masks, home_ref, *refs):
    for marks, out in zip(refs[: len(refs) // 2], refs[len(refs) // 2 :]):
        rows = marks.shape[0]
        size, height = TILE // cap * rows, out.shape[1]
        repeated = tiled(marks[...], cap)
        lane, _ = block_lanes((height, LANES), 0, cap, masks, home_ref[0])
        part = iota((size, height), 1) % TILE // cap
        same = part == iota((size, height), 0) // rows
        for k in range(3):
            wanted = lane + (k + 1) * (LANES // 4) == iota((height, LANES), 1)
            term = lanes_dot(repeated, jnp.where(wanted, 1.0, 0.0).astype(BF16))
            out[k * size : (k + 1) * size, :] = jnp.where(same, term, 0.0).astype(BF16)


def combine_kernel(cap, count, share_ref, *refs):
    blocks, sums, out = refs[:count], refs[count:-1], refs[-1]
    rows = out.shape[0]
    parts = TILE // cap
    width = out.shape[1] // parts
    arrived = jnp.concatenate([b[...] for b in blocks], axis=0)
    terms = matmul(share_ref[...], arrived)
    size = parts * rows
    routed = terms[:size] + terms[size : 2 * size] + terms[2 * size :]
    for q in range(parts):
        here = slice(q * width, (q + 1) * width)
        total = routed[q * rows : (q + 1) * rows]
        for part in sums:
            total += part[:, here].astype(F32)
        out[:, here] = total.astype(out.dtype)


def on_device(
    tokens,
    expert_ids,
    gate_weights,
    w_gate,
    scale_gate,
    w_up,
    scale_up,
    w_down,
    scale_down,
    outlier_cols,
    outlier_gate,
    outlier_up,
    shared_gate,
    shared_up,
    shared_down,
):
    devices = lax.axis_size("ep")
    device = lax.axis_index("ep")
    hid = w_gate.shape[2]
    group = FF // hid
    experts = devices // group
    bits = group.bit_length() - 1
    rows, width = tokens.shape[1], tokens.shape[2]
    cap = max(2, rows * TOPK * 2 // experts)
    home = device // group
    part_width = width * cap // TILE
    slots = experts * cap

    def swap(array, mask):
        return lax.ppermute(array, "ep", [(d, d ^ mask) for d in range(devices)])

    def spread(pieces):
        for bit in range(bits):
            pieces = pieces + [swap(piece, 1 << bit) for piece in pieces]
        return pieces

    current = tokens[0]
    ids, weights = expert_ids[0].T, gate_weights[0].T
    home_ref = home.astype(jnp.int32).reshape(1)
    masks = list(range(experts))

    parts = TILE // cap
    sent_block = jax.ShapeDtypeStruct((TILE, part_width), BF16)
    stack = pltpu.VMEM((parts * rows, part_width), F32)
    marks, *blocks = pl.pallas_call(
        functools.partial(first_kernel, cap, masks),
        in_specs=[SMEM] + [ANY] * 3,
        out_specs=[VMEM] * (1 + experts),
        out_shape=[jax.ShapeDtypeStruct((rows, LANES), BF16)] + [sent_block] * experts,
        scratch_shapes=[
            pltpu.SMEM(ids.shape, jnp.int32),
            pltpu.SMEM(weights.shape, F32),
            pltpu.VMEM((rows, width), BF16),
            stack,
            pltpu.SemaphoreType.DMA((3,)),
        ],
        compiler_params=params(8),
        cost_estimate=cost(AHEAD, 1e6),
        name="first",
    )(home_ref, in_hbm(ids), in_hbm(weights), in_hbm(current))
    def exchanged(blocks):
        return [swap(block, mask * group) if mask else block for mask, block in zip(masks, blocks)]

    arrived = exchanged(blocks)

    step = 1024
    cols, rows_here, _ = lax.optimization_barrier(
        (lax.dynamic_slice_in_dim(outlier_cols, home, 1, 0), current, blocks[0])
    )
    early = [w_gate[0], w_up[0], shared_gate[0], shared_up[0]]
    onehot, keep = pl.pallas_call(
        functools.partial(outlier_kernel, step),
        in_specs=[VMEM] * (1 + len(early)),
        out_specs=[VMEM] * 2,
        out_shape=[
            jax.ShapeDtypeStruct((width, outlier_cols.shape[1]), BF16),
            jax.ShapeDtypeStruct((8, width), F32),
        ],
        compiler_params=params(8),
        cost_estimate=cost(1e8, 1e6),
        name="outlier",
    )(cols, *early)
    row_pieces = spread([rows_here])
    hidden = pl.pallas_call(
        functools.partial(shared_up_kernel, step),
        in_specs=[VMEM] * (2 + group),
        out_specs=VMEM,
        out_shape=jax.ShapeDtypeStruct((group * rows, hid), BF16),
        scratch_shapes=[
            pltpu.VMEM((group * rows, width), BF16),
            pltpu.VMEM((group * rows, hid), F32),
            pltpu.VMEM((group * rows, hid), F32),
        ],
        compiler_params=params(8),
        cost_estimate=cost(4 * group * rows * width * hid, 4 * hid * width),
        name="shared_up",
    )(shared_gate[0], shared_up[0], *row_pieces)
    arrived, keep, hidden = lax.optimization_barrier((arrived, keep, hidden))

    whole = jax.ShapeDtypeStruct((slots, width), BF16)
    taken = pl.pallas_call(
        functools.partial(unpack_kernel, cap),
        in_specs=[VMEM] * len(arrived),
        out_specs=VMEM,
        out_shape=whole,
        compiler_params=params(10),
        cost_estimate=cost(1e8, 1e6),
        name="unpack",
    )(*arrived)
    pieces = spread([taken])

    hidden, marks, _ = lax.optimization_barrier((hidden, marks, taken))
    shared = pl.pallas_call(
        functools.partial(shared_down_kernel, 1024),
        in_specs=[VMEM] * 2,
        out_specs=[VMEM] * group,
        out_shape=[jax.ShapeDtypeStruct((rows, width), F32)]
        + [jax.ShapeDtypeStruct((rows, width), BF16)] * (group - 1),
        compiler_params=params(8),
        cost_estimate=cost(2 * group * rows * width * hid, 2 * hid * width),
        name="shared_down",
    )(hidden, shared_down[0])
    shares = pl.pallas_call(
        functools.partial(share_kernel, cap, masks),
        in_specs=[SMEM, VMEM],
        out_specs=[VMEM],
        out_shape=[jax.ShapeDtypeStruct((3 * parts * rows, experts * TILE), BF16)],
        compiler_params=params(4),
        cost_estimate=cost(1e6, 1e5),
        name="share",
    )(home_ref, marks)
    pieces, shares, shared = lax.optimization_barrier((pieces, shares, shared))

    partials = pl.pallas_call(
        functools.partial(expert_kernel, step, 1024, group),
        in_specs=[VMEM, VMEM, ANY] + [VMEM] * (7 + group),
        out_specs=[VMEM] * group,
        out_shape=[whole] * group,
        scratch_shapes=[
            pltpu.VMEM((hid, width), BF16),
            pltpu.VMEM((group * slots, hid), F32),
            pltpu.VMEM((group * slots, hid), F32),
            pltpu.VMEM((group * slots, outlier_cols.shape[1]), F32),
            pltpu.VMEM((group * slots, hid), BF16),
            pltpu.VMEM(scale_gate.shape[1:], F32),
            pltpu.VMEM(scale_up.shape[1:], F32),
            pltpu.VMEM(scale_down.shape[1:], F32),
            pltpu.SemaphoreType.DMA,
        ],
        compiler_params=params(10),
        cost_estimate=cost(6 * group * slots * width * hid, 6 * hid * width),
        name="expert",
    )(
        w_gate[0],
        w_up[0],
        in_hbm(w_down[0]),
        onehot,
        keep,
        scale_gate[0],
        scale_up[0],
        scale_down[0],
        outlier_gate[0],
        outlier_up[0],
        *pieces,
    )

    for bit in reversed(range(1, bits)):
        half = 1 << bit
        partials = [
            (mine.astype(F32) + swap(other, half).astype(F32)).astype(BF16)
            for mine, other in zip(partials[:half], partials[half:])
        ]
    returning = pl.pallas_call(
        functools.partial(pack_kernel, cap),
        in_specs=[VMEM] * 2,
        out_specs=[VMEM] * experts,
        out_shape=[sent_block] * experts,
        compiler_params=params(10),
        cost_estimate=cost(1e8, 1e6),
        name="pack",
    )(partials[0], swap(partials[1], 1))
    returned = exchanged(returning)
    sums = [shared[0]] + [swap(shared[n], n) for n in range(1, group)]
    out = pl.pallas_call(
        functools.partial(combine_kernel, cap, experts),
        in_specs=[VMEM] * (1 + experts + group),
        out_specs=VMEM,
        out_shape=jax.ShapeDtypeStruct((rows, width), BF16),
        compiler_params=params(10),
        cost_estimate=cost(1e8, 1e6),
        name="combine",
    )(*shares, *returned, *sums)
    return out[None]


def solution(mesh):
    rows = P(None, ("parts", "ep"), None)
    held = P("ep", None, None)
    placed = (rows, rows, rows) + (held,) * 6 + (P(),) + (held,) * 5
    return jax.shard_map(
        on_device, mesh=mesh, in_specs=placed, out_specs=rows, check_vma=False
    )
```
